32 devices in a mesh: section: 2 (over y), dp: 16 (over z, x, core).
Axes of the slice: x: 2, y: 2, z: 4, core: 2. Of those that a mesh axis runs over, the one named last changes fastest.
Arguments:
- chars: bfloat16 [8192, 16, 256], P('dp'), may hold values from -6 to 6
- char_lengths: int32 [8192], P('dp'), may hold values from 1 to 16, as said below
- word_mask: int32 [8192], P('dp'), may hold values from 0 to 1, as said below
- out_grad: bfloat16 [8192, 512], P('dp'), may hold values from -6 to 6
- char_gain_a: bfloat16 [256], replicated, may hold values from 0.5 to 1.5
- char_qkv: bfloat16 [256, 768], replicated, may hold values from -0.375 to 0.375
- char_out: bfloat16 [256, 256], replicated, may hold values from -0.75 to 0.75
- char_gain_b: bfloat16 [256], replicated, may hold values from 0.5 to 1.5
- char_up: bfloat16 [256, 1024], replicated, may hold values from -0.375 to 0.375
- char_down: bfloat16 [1024, 256], replicated, may hold values from -0.25 to 0.25
- pool_gain: bfloat16 [256], replicated, may hold values from 0.5 to 1.5
- pool_query: bfloat16 [256], replicated, may hold values from -12 to 12
- char_proj: bfloat16 [256, 512], replicated, may hold values from -0.375 to 0.375
- word_gain_a: bfloat16 [512], replicated, may hold values from 0.5 to 1.5
- word_qkv: bfloat16 [512, 1536], replicated, may hold values from -0.25 to 0.25
- word_out: bfloat16 [512, 512], replicated, may hold values from -1.5 to 1.5
- word_gain_b: bfloat16 [512], replicated, may hold values from 0.5 to 1.5
- word_up: bfloat16 [512, 2048], replicated, may hold values from -0.25 to 0.25
- word_down: bfloat16 [2048, 512], replicated, may hold values from -0.1875 to 0.1875
Outputs:
- word_outputs: bfloat16 [8192, 512], P('dp', 'section')
- char_grad: bfloat16 [8192, 16, 256], P('dp', None, 'section')
- char_gain_a_grad: float32 [256], replicated
- char_qkv_grad: float32 [256, 768], replicated
- char_out_grad: float32 [256, 256], replicated
- char_gain_b_grad: float32 [256], replicated
- char_up_grad: float32 [256, 1024], replicated
- char_down_grad: float32 [1024, 256], replicated
- pool_gain_grad: float32 [256], replicated
- pool_query_grad: float32 [256], replicated
- char_proj_grad: float32 [256, 512], replicated
- word_gain_a_grad: float32 [512], replicated
- word_qkv_grad: float32 [512, 1536], replicated
- word_out_grad: float32 [512, 512], replicated
- word_gain_b_grad: float32 [512], replicated
- word_up_grad: float32 [512, 2048], replicated
- word_down_grad: float32 [2048, 512], replicated
The draws below stay inside these ranges and needn't reach their ends.
Inputs may be any that keep to these rules, and one draw needn't show every extreme that they name: `char_lengths`: every word has at least one character; some word has all 16. `word_mask`: within each sequence the ones form a prefix that starts at its first word and covers at least half of it; at least one sequence has no padding.
All inputs are finite; a program needn't handle non-finite values.
Results may differ from the reference program's by a relative error of at most 0.023.
Values may be sent and summed in bfloat16 or wider, within the bound.
No kernel may reach another device: no remote copies, remote signals or barrier semaphores. Data moves between devices by JAX's collectives and lax.ppermute only.
A program may use at most 256 MiB of HBM per device.

```python
import jax
import jax.numpy as jnp
from jax import lax

CWIDTH = 256
CHEADS = 4
CHIDDEN = 1024
WWIDTH = 512
WHEADS = 8
WHIDDEN = 2048
CHARS = 16
TOKENS = 8192
SEQS = 32
LENGTH = 256


def draw_char_lengths(key, part):
    key = jax.random.fold_in(key, 11)
    subkeys = jax.random.split(key, 4)
    base_len = jax.random.randint(subkeys[0], (TOKENS,), 1, max(2, CHARS // 4) + 1)
    tail_hit = jax.random.randint(subkeys[1], (TOKENS,), 0, 4) == 0
    extra_len = jax.random.randint(subkeys[2], (TOKENS,), 0, CHARS)
    lengths = jnp.minimum(base_len + jnp.where(tail_hit, extra_len, 0), CHARS)
    full_spot = jax.random.randint(subkeys[3], (), 0, TOKENS)
    return lengths.at[full_spot].set(CHARS).astype(jnp.int32)


def draw_word_mask(key, part):
    key = jax.random.fold_in(key, 23)
    subkeys = jax.random.split(key, 3)
    padded = jax.random.randint(subkeys[0], (SEQS,), 0, 3) == 0
    cut_len = jax.random.randint(subkeys[1], (SEQS,), 0, LENGTH // 2)
    cut_len = jnp.where(padded, cut_len, 0)
    full_seq = jax.random.randint(subkeys[2], (), 0, SEQS)
    cut_len = jnp.where(jnp.arange(SEQS) == full_seq, 0, cut_len)
    position = jnp.arange(LENGTH)[None, :]
    table = (position < (LENGTH - cut_len)[:, None]).astype(jnp.int32)
    return table.reshape(TOKENS).astype(jnp.int32)


def level_of(rng, dims, shards, low, high):
    level, own = 1.0, jax.random.fold_in(rng, 6)
    for dim, blocks in shards:
        heights = jnp.exp(jax.random.uniform(jax.random.fold_in(own, dim), (blocks,), jnp.float32, low / len(shards), high / len(shards)))
        level = level * jnp.repeat(heights, dims[dim] // blocks).reshape([-1 if axis == dim else 1 for axis in range(len(dims))])
    return level


def bell_draw(stream_key, dims, scale, reach, pieces=(), kind=jnp.bfloat16):
    values = scale * jax.random.normal(stream_key, dims, jnp.float32)
    if pieces:
        values = values * level_of(stream_key, dims, pieces, -0.22, 0.18)
    return jnp.clip(values, -reach, reach).astype(kind)


def setup_inputs(seed: int = 0) -> dict:
    keys = jax.random.split(jax.random.key(seed), 20)
    chars = bell_draw(keys[0], (TOKENS, CHARS, CWIDTH), 1.0, 6.0, ((0, 16),))
    char_lengths = draw_char_lengths(jax.random.fold_in(keys[19], 71), 0)
    word_mask = draw_word_mask(jax.random.fold_in(keys[19], 71), 0)
    out_grad = bell_draw(keys[3], (TOKENS, WWIDTH), 1.0, 6.0, ((0, 16),))
    char_gain_a = jnp.clip(1.0 + 0.1 * jax.random.normal(keys[4], (CWIDTH,), jnp.float32), 0.5, 1.5).astype(jnp.bfloat16)
    char_qkv = bell_draw(keys[5], (CWIDTH, 3 * CWIDTH), CWIDTH ** -0.5, 0.375)
    char_out = bell_draw(keys[6], (CWIDTH, CWIDTH), (CWIDTH // 4) ** -0.5, 0.75)
    char_gain_b = jnp.clip(1.0 + 0.1 * jax.random.normal(keys[7], (CWIDTH,), jnp.float32), 0.5, 1.5).astype(jnp.bfloat16)
    char_up = bell_draw(keys[8], (CWIDTH, CHIDDEN), CWIDTH ** -0.5, 0.375)
    char_down = bell_draw(keys[9], (CHIDDEN, CWIDTH), (CHIDDEN // 2) ** -0.5, 0.25)
    pool_gain = jnp.clip(1.0 + 0.1 * jax.random.normal(keys[10], (CWIDTH,), jnp.float32), 0.5, 1.5).astype(jnp.bfloat16)
    pool_query = bell_draw(keys[11], (CWIDTH,), 2.0, 12.0)
    char_proj = bell_draw(keys[12], (CWIDTH, WWIDTH), CWIDTH ** -0.5, 0.375)
    word_gain_a = jnp.clip(1.0 + 0.1 * jax.random.normal(keys[13], (WWIDTH,), jnp.float32), 0.5, 1.5).astype(jnp.bfloat16)
    word_qkv = bell_draw(keys[14], (WWIDTH, 3 * WWIDTH), WWIDTH ** -0.5, 0.25)
    word_out = bell_draw(keys[15], (WWIDTH, WWIDTH), (WWIDTH // 32) ** -0.5, 1.5)
    word_gain_b = jnp.clip(1.0 + 0.1 * jax.random.normal(keys[16], (WWIDTH,), jnp.float32), 0.5, 1.5).astype(jnp.bfloat16)
    word_up = bell_draw(keys[17], (WWIDTH, WHIDDEN), WWIDTH ** -0.5, 0.25)
    word_down = bell_draw(keys[18], (WHIDDEN, WWIDTH), (WHIDDEN // 2) ** -0.5, 0.1875)
    return {"chars": chars, "char_lengths": char_lengths, "word_mask": word_mask, "out_grad": out_grad, "char_gain_a": char_gain_a, "char_qkv": char_qkv, "char_out": char_out, "char_gain_b": char_gain_b, "char_up": char_up, "char_down": char_down, "pool_gain": pool_gain, "pool_query": pool_query, "char_proj": char_proj, "word_gain_a": word_gain_a, "word_qkv": word_qkv, "word_out": word_out, "word_gain_b": word_gain_b, "word_up": word_up, "word_down": word_down}


EPSILON = 1e-06
NEGATIVE = -1e+30
HIGH = lax.Precision.HIGHEST

@jax.custom_vjp
def low(v):
    return lax.optimization_barrier(v.astype(jnp.bfloat16)).astype(jnp.float32)

@jax.custom_vjp
def low_back(v):
    return v

def low_keep(v):
    return (low(v), None)

def low_pass(kept, grad):
    return (grad,)

def back_keep(v):
    return (v, None)

def back_low(kept, grad):
    return (low(grad),)
low.defvjp(low_keep, low_pass)
low_back.defvjp(back_keep, back_low)

def both_ways(value):
    return low(low_back(value))

def matmul(left, right):
    return jnp.dot(left, right, precision=HIGH)

def rms_scale(value, gain):
    return value * lax.rsqrt(lax.optimization_barrier(jnp.mean(value * value, axis=-1, keepdims=True)) + EPSILON) * gain

def pool_words(states, gain, query, valid):
    normed = rms_scale(states, gain)
    score = lax.optimization_barrier(jnp.sum(normed * query, axis=-1)) * states.shape[-1] ** (-0.5)
    score = jnp.where(valid, score, NEGATIVE)
    weights = jax.nn.softmax(score, axis=-1)
    return lax.optimization_barrier(jnp.sum(weights[..., None] * normed, axis=-2))

def char_block(params, chars, lens):
    gain_a, w_qkv, w_out, gain_b, w_up, w_down, gain_p, query_p, w_proj = params
    words, count, width = chars.shape
    size = width // CHEADS
    valid = lax.broadcasted_iota(jnp.int32, (words, count), 1) < lens[:, None]
    low_a = low(rms_scale(chars, gain_a))
    qkv = both_ways(matmul(low_a, w_qkv)).reshape(words, count, 3, CHEADS, size)
    score = jnp.einsum('wqhd,wkhd->whqk', qkv[:, :, 0], qkv[:, :, 1], precision=HIGH) * size ** (-0.5)
    score = low_back(jnp.where(valid[:, None, None, :], score, NEGATIVE))
    probs = low(jax.nn.softmax(score, axis=-1))
    mixed = jnp.einsum('whqk,wkhd->wqhd', probs, qkv[:, :, 2], precision=HIGH).reshape(words, count, width)
    mixed = both_ways(mixed)
    after_a = chars + low_back(matmul(mixed, w_out))
    low_b = low(rms_scale(after_a, gain_b))
    pre_act = low_back(matmul(low_b, w_up))
    hidden = low(jax.nn.gelu(pre_act))
    after_b = after_a + low_back(matmul(hidden, w_down))
    pooled = low(pool_words(after_b, gain_p, query_p, valid))
    return both_ways(matmul(pooled, w_proj))

def word_block(params, vector, mask):
    gain_c, w_qkv, w_out, gain_d, w_up, w_down = params
    length, width = vector.shape
    size = width // WHEADS
    low_c = low(rms_scale(vector, gain_c))
    qkv = both_ways(matmul(low_c, w_qkv)).reshape(length, 3, WHEADS, size)
    score = jnp.einsum('qhd,khd->hqk', qkv[:, 0], qkv[:, 1], precision=HIGH) * size ** (-0.5)
    place = lax.broadcasted_iota(jnp.int32, (length, length), 0)
    other = lax.broadcasted_iota(jnp.int32, (length, length), 1)
    allowed = (other <= place) & (mask[None, :] > 0)
    score = low_back(jnp.where(allowed[None], score, NEGATIVE))
    probs = low(jax.nn.softmax(score, axis=-1))
    mixed = both_ways(jnp.einsum('hqk,khd->qhd', probs, qkv[:, 2], precision=HIGH).reshape(length, width))
    after_a = vector + low_back(matmul(mixed, w_out))
    low_d = low(rms_scale(after_a, gain_d))
    pre_act = low_back(matmul(low_d, w_up))
    hidden = low(jax.nn.gelu(pre_act))
    return after_a + low_back(matmul(hidden, w_down))

def to_sequences(array):
    return array.reshape((SEQS, LENGTH) + array.shape[1:])

def from_sequences(array):
    return array.reshape((TOKENS,) + array.shape[2:])

def reference(chars, char_lengths, word_mask, out_grad, char_gain_a, char_qkv, char_out, char_gain_b, char_up, char_down, pool_gain, pool_query, char_proj, word_gain_a, word_qkv, word_out, word_gain_b, word_up, word_down):
    char_params = tuple((w.astype(jnp.float32) for w in (char_gain_a, char_qkv, char_out, char_gain_b, char_up, char_down, pool_gain, pool_query, char_proj)))
    word_params = tuple((w.astype(jnp.float32) for w in (word_gain_a, word_qkv, word_out, word_gain_b, word_up, word_down)))
    chars_seq = to_sequences(chars.astype(jnp.float32))
    lens_seq = to_sequences(char_lengths)
    mask_seq = to_sequences(word_mask)

    def one_sequence(char_p, word_p, chars_one, lens_one, mask_one):
        vector = char_block(char_p, chars_one, lens_one)
        return word_block(word_p, vector, mask_one)
    saved = jax.checkpoint(one_sequence)

    def forward(char_p, word_p, chars_all):

        def step(carry, item):
            return (carry, saved(char_p, word_p, item[0], item[1], item[2]))
        return lax.scan(step, jnp.zeros((), jnp.float32), (chars_all, lens_seq, mask_seq))[1]
    result, pullback = jax.vjp(forward, char_params, word_params, chars_seq)
    d_char, d_word, d_chars = pullback(to_sequences(out_grad.astype(jnp.float32)))
    return (from_sequences(result).astype(jnp.bfloat16), from_sequences(d_chars).astype(jnp.bfloat16), d_char[0], d_char[1], d_char[2], d_char[3], d_char[4], d_char[5], d_char[6], d_char[7], d_char[8], d_word[0], d_word[1], d_word[2], d_word[3], d_word[4], d_word[5])
```

```python
import functools

import jax
import jax.numpy as jnp
from jax import lax
from jax.experimental import pallas as pl
from jax.experimental.pallas import tpu as pltpu
from jax.sharding import PartitionSpec as P

CHEADS = 4
WHEADS = 8
EPSILON = 1e-06
NEGATIVE = -1e30
BLOCK_WORDS = 32
GROUP = 128
F32 = jnp.float32
BF16 = jnp.bfloat16
C0 = 0.7978845608028654
C1 = 0.7978845608028654 * 0.044715


def mm(left, right):
    return jnp.dot(left, right, preferred_element_type=F32)


def mm_nt(left, right):
    return lax.dot_general(left, right, (((1,), (1,)), ((), ())), preferred_element_type=F32)


def mm_tn(left, right):
    return lax.dot_general(left, right, (((0,), (0,)), ((), ())), preferred_element_type=F32)


def inverse_rms(value):
    return lax.rsqrt(jnp.mean(value * value, axis=-1, keepdims=True) + EPSILON)


def gelu(u):
    t = jnp.tanh(u * (C0 + C1 * (u * u)))
    half = 0.5 * u
    return half + half * t


def gelu_both(u):
    square = u * u
    t = jnp.tanh(u * (C0 + C1 * square))
    half = 0.5 * u
    slope = (0.5 + 0.5 * t) + half * (1.0 - t * t) * (C0 + (3.0 * C1) * square)
    return half + half * t, slope


def rms_back(unit, inverse, gain, grad):
    scaled = grad * gain
    d_value = inverse * (scaled - unit * jnp.mean(scaled * unit, axis=-1, keepdims=True))
    return d_value, jnp.sum(grad * unit, axis=0, keepdims=True)


def two_heads(pair):
    lane = lax.broadcasted_iota(jnp.int32, pair.shape, 1)
    zero = jnp.zeros_like(pair)
    return jnp.concatenate(
        [jnp.where(lane < 64, pair, zero), jnp.where(lane < 64, zero, pair)], axis=0
    )


def side(stacked):
    n = stacked.shape[0] // 2
    return jnp.concatenate([stacked[:n], stacked[n:]], axis=1)


def pool_forward(x2, gain, query, lens_rows):
    rows, width = x2.shape
    inverse = inverse_rms(x2)
    unit = x2 * inverse
    normed = unit * gain
    score = jnp.sum(normed * query, axis=-1, keepdims=True) * width ** (-0.5)
    words = rows // 16
    place = lax.broadcasted_iota(jnp.int32, (rows, 1), 0) % 16
    score = jnp.where(place < lens_rows, score, NEGATIVE)
    score = score.reshape(words, 16, 1)
    exps = jnp.exp(score - jnp.max(score, axis=1, keepdims=True))
    weights = exps / jnp.sum(exps, axis=1, keepdims=True)
    return inverse, unit, normed, weights


def lens_column(lens):
    row = lax.broadcasted_iota(jnp.int32, (GROUP, GROUP), 0)
    lane = lax.broadcasted_iota(jnp.int32, (GROUP, GROUP), 1)
    pick = row == lane
    out = []
    for g in range(lens.shape[0]):
        out.append(jnp.sum(jnp.where(pick, lens[g : g + 1], 0), axis=1, keepdims=True))
    return jnp.concatenate(out, axis=0)


def char_forward_kernel(
    sec_ref, chars, lens, gain_a, w_qkv, w_out, gain_b, w_up, w_down, gain_p, query_p, w_proj,
    qkv_out, o1_out, x1_out, u1_out, x2_out, pooled_out, e_out,
):
    words, slots, width = chars.shape
    rows = words * slots
    x = chars[...].reshape(rows, width).astype(F32)
    a1 = (x * inverse_rms(x) * gain_a[...].astype(F32)).astype(BF16)
    qkv_out[...] = mm(a1, w_qkv[...]).astype(BF16)
    row = lax.broadcasted_iota(jnp.int32, (GROUP, GROUP), 0)
    lane = lax.broadcasted_iota(jnp.int32, (GROUP, GROUP), 1)
    same = (row // 16) == (lane // 16)
    lens_now = lens[0]
    for g in range(rows // GROUP):
        at = slice(g * GROUP, (g + 1) * GROUP)
        allowed = same & ((lane % 16) < lens_now[g : g + 1])
        mask = jnp.where(allowed, 0.0, NEGATIVE)
        mask = jnp.concatenate([mask, mask], axis=0)
        for j in range(2):
            q = qkv_out[at, j * 128 : j * 128 + 128] * 0.125
            k = qkv_out[at, width + j * 128 : width + j * 128 + 128]
            v = qkv_out[at, 2 * width + j * 128 : 2 * width + j * 128 + 128]
            s = mm_nt(two_heads(q), k) + mask
            e = jnp.exp(s - jnp.max(s, axis=-1, keepdims=True))
            p = (e / jnp.sum(e, axis=-1, keepdims=True)).astype(BF16)
            o1_out[at, j * 128 : j * 128 + 128] = mm(side(p), two_heads(v)).astype(BF16)
    x1 = x + mm(o1_out[...], w_out[...])
    x1_out[...] = x1
    a2 = (x1 * inverse_rms(x1) * gain_b[...].astype(F32)).astype(BF16)
    u1 = mm(a2, w_up[...])
    u1_out[...] = u1.astype(BF16)
    h1 = gelu(u1).astype(BF16)
    x2 = x1 + mm(h1, w_down[...])
    x2_out[...] = x2
    _, _, normed, weights = pool_forward(
        x2, gain_p[...].astype(F32), query_p[...].astype(F32), lens_column(lens_now)
    )
    pooled = jnp.sum(weights * normed.reshape(words, 16, width), axis=1).astype(BF16)
    pooled_out[...] = pooled
    e_out[...] = mm(pooled, w_proj[...]).astype(BF16)


def word_kernel(
    e_ref, mask_ref, g_ref, pooled_ref, gain_c, w_qkv, w_out, gain_d, w_up, w_down, w_proj,
    out_ref, grads_ref, gains_ref, proj_ref, gpool_ref,
):
    rows, width = e_ref.shape
    hidden = w_up.shape[1]
    y = e_ref[...].astype(F32)
    gain_c_f = gain_c[...].astype(F32)
    gain_d_f = gain_d[...].astype(F32)
    inv_c = inverse_rms(y)
    unit_c = y * inv_c
    a3 = (unit_c * gain_c_f).astype(BF16)
    qkv = mm(a3, w_qkv[...]).astype(BF16)
    row = lax.broadcasted_iota(jnp.int32, (rows, rows), 0)
    lane = lax.broadcasted_iota(jnp.int32, (rows, rows), 1)
    allowed = (lane <= row) & (mask_ref[...] > 0)
    mask = jnp.where(allowed, 0.0, NEGATIVE)
    mask = jnp.concatenate([mask, mask], axis=0)
    pairs = width // 128
    probs, mixed = [], []
    for j in range(pairs):
        q = qkv[:, j * 128 : j * 128 + 128] * 0.125
        k = qkv[:, width + j * 128 : width + j * 128 + 128]
        v = qkv[:, 2 * width + j * 128 : 2 * width + j * 128 + 128]
        s = mm_nt(two_heads(q), k) + mask
        e = jnp.exp(s - jnp.max(s, axis=-1, keepdims=True))
        p = e / jnp.sum(e, axis=-1, keepdims=True)
        probs.append(p)
        mixed.append(mm(side(p.astype(BF16)), two_heads(v)).astype(BF16))
    o2 = jnp.concatenate(mixed, axis=1)
    y1 = y + mm(o2, w_out[...])
    inv_d = inverse_rms(y1)
    unit_d = y1 * inv_d
    a4 = (unit_d * gain_d_f).astype(BF16)
    u2 = mm(a4, w_up[...])
    h2, slope = gelu_both(u2)
    h2 = h2.astype(BF16)
    out_ref[...] = (y1 + mm(h2, w_down[...])).astype(BF16)
    g = g_ref[...]
    grads_ref[0:hidden, :] = mm_tn(h2, g).astype(BF16)
    g_u2 = (slope * mm_nt(g, w_down[...])).astype(BF16)
    at = hidden
    for j in range(hidden // width):
        grads_ref[at : at + width, :] = mm_tn(a4, g_u2[:, j * width : (j + 1) * width]).astype(BF16)
        at += width
    d_y1n, d_gain_d = rms_back(unit_d, inv_d, gain_d_f, mm_nt(g_u2, w_up[...]))
    g_y1 = g.astype(F32) + d_y1n
    g_b1 = g_y1.astype(BF16)
    grads_ref[at : at + width, :] = mm_tn(o2, g_b1).astype(BF16)
    at += width
    g_o2 = mm_nt(g_b1, w_out[...]).astype(BF16)
    d_q, d_k, d_v = [], [], []
    for j in range(pairs):
        q = qkv[:, j * 128 : j * 128 + 128] * 0.125
        k = qkv[:, width + j * 128 : width + j * 128 + 128]
        v = qkv[:, 2 * width + j * 128 : 2 * width + j * 128 + 128]
        go = two_heads(g_o2[:, j * 128 : j * 128 + 128])
        p = probs[j]
        g_p = mm_nt(go, v)
        d_v.append(mm_tn(p.astype(BF16), go).astype(BF16))
        d_s = (p * (g_p - jnp.sum(g_p * p, axis=-1, keepdims=True))).astype(BF16)
        d_q.append((mm(side(d_s), two_heads(k)) * 0.125).astype(BF16))
        d_k.append(mm_tn(d_s, two_heads(q)).astype(BF16))
    g_qkv = jnp.concatenate(d_q + d_k + d_v, axis=1)
    for j in range(3):
        grads_ref[at : at + width, :] = mm_tn(a3, g_qkv[:, j * width : (j + 1) * width]).astype(BF16)
        at += width
    d_yn, d_gain_c = rms_back(unit_c, inv_c, gain_c_f, mm_nt(g_qkv, w_qkv[...]))
    g_e = (g_y1 + d_yn).astype(BF16)
    gains_ref[0:1, :] = d_gain_c
    gains_ref[1:2, :] = d_gain_d
    gains_ref[2:8, :] = jnp.zeros((6, width), F32)
    proj_ref[...] = mm_tn(pooled_ref[...], g_e).astype(BF16)
    gpool_ref[...] = mm_nt(g_e, w_proj[...])


def char_backward_kernel(
    sec_ref, chars, lens, gpool, qkv_in, o1_in, x1_in, u1_in, x2_in,
    gain_a, w_qkv, w_out, gain_b, w_up, w_down, gain_p, query_p,
    own_ref, send_ref, grads_ref, gains_ref,
    acc_down, acc_up, acc_out, acc_qkv, acc_gain,
):
    step = pl.program_id(0)
    words, slots, width = chars.shape
    rows = words * slots
    hidden = w_up.shape[1]

    @pl.when(step == 0)
    def _():
        acc_down[...] = jnp.zeros_like(acc_down)
        acc_up[...] = jnp.zeros_like(acc_up)
        acc_out[...] = jnp.zeros_like(acc_out)
        acc_qkv[...] = jnp.zeros_like(acc_qkv)
        acc_gain[...] = jnp.zeros_like(acc_gain)

    lens_now = lens[0]
    gain_pf = gain_p[...].astype(F32)
    query = query_p[...].astype(F32)
    x2 = x2_in[...]
    inv_p, unit_p, normed, weights = pool_forward(x2, gain_pf, query, lens_column(lens_now))
    normed3 = normed.reshape(words, 16, width)
    gp = gpool[...].reshape(words, 1, width)
    g_w = jnp.sum(normed3 * gp, axis=-1, keepdims=True)
    g_r = weights * (g_w - jnp.sum(g_w * weights, axis=1, keepdims=True)) * width ** (-0.5)
    g_n = (weights * gp + g_r * query.reshape(1, 1, width)).reshape(rows, width)
    d_query = jnp.sum((g_r * normed3).reshape(rows, width), axis=0, keepdims=True)
    g_x2, d_gain_p = rms_back(unit_p, inv_p, gain_pf, g_n)
    g_b2 = g_x2.astype(BF16)
    h1, slope = gelu_both(u1_in[...].astype(F32))
    acc_down[...] += mm_tn(g_b2, h1.astype(BF16))
    g_u1 = (slope * mm_nt(g_b2, w_down[...])).astype(BF16)
    gain_bf = gain_b[...].astype(F32)
    x1 = x1_in[...]
    inv_b = inverse_rms(x1)
    unit_b = x1 * inv_b
    acc_up[...] += mm_tn((unit_b * gain_bf).astype(BF16), g_u1)
    d_x1n, d_gain_b = rms_back(unit_b, inv_b, gain_bf, mm_nt(g_u1, w_up[...]))
    g_x1 = g_x2 + d_x1n
    g_c1 = g_x1.astype(BF16)
    acc_out[...] += mm_tn(o1_in[...], g_c1)
    g_o1 = mm_nt(g_c1, w_out[...]).astype(BF16)
    row = lax.broadcasted_iota(jnp.int32, (GROUP, GROUP), 0)
    lane = lax.broadcasted_iota(jnp.int32, (GROUP, GROUP), 1)
    same = (row // 16) == (lane // 16)
    parts = []
    for g in range(rows // GROUP):
        at = slice(g * GROUP, (g + 1) * GROUP)
        allowed = same & ((row % 16) < lens_now[g : g + 1])
        mask = jnp.where(allowed, 0.0, NEGATIVE)
        d_q, d_k, d_v = [], [], []
        for j in range(2):
            q = qkv_in[at, j * 128 : j * 128 + 128] * 0.125
            k = qkv_in[at, width + j * 128 : width + j * 128 + 128]
            v = qkv_in[at, 2 * width + j * 128 : 2 * width + j * 128 + 128]
            go = g_o1[at, j * 128 : j * 128 + 128]
            ks = two_heads(k)
            s = mm_nt(ks, q).reshape(2, GROUP, GROUP) + mask
            e = jnp.exp(s - jnp.max(s, axis=1, keepdims=True))
            p = e * (1.0 / jnp.sum(e, axis=1, keepdims=True))
            g_p = mm_nt(two_heads(v), go).reshape(2, GROUP, GROUP)
            d_s = p * (g_p - jnp.sum(g_p * p, axis=1, keepdims=True))
            d_s = d_s.astype(BF16).reshape(2 * GROUP, GROUP)
            p_low = p.astype(BF16).reshape(2 * GROUP, GROUP)
            d_v.append(mm(side(p_low), two_heads(go)).astype(BF16))
            d_k.append(mm(side(d_s), two_heads(q)).astype(BF16))
            d_q.append((mm_tn(d_s, ks) * 0.125).astype(BF16))
        parts.append(jnp.concatenate(d_q + d_k + d_v, axis=1))
    g_qkv = jnp.concatenate(parts, axis=0)
    gain_af = gain_a[...].astype(F32)
    x = chars[...].reshape(rows, width).astype(F32)
    inv_a = inverse_rms(x)
    unit_a = x * inv_a
    acc_qkv[...] += mm_tn((unit_a * gain_af).astype(BF16), g_qkv)
    d_xn, d_gain_a = rms_back(unit_a, inv_a, gain_af, mm_nt(g_qkv, w_qkv[...]))
    d_chars = (g_x1 + d_xn).astype(BF16).reshape(words, slots, width)
    first = sec_ref[0] == 0
    left, right = d_chars[:, :, : width // 2], d_chars[:, :, width // 2 :]

    @pl.when(first)
    def _():
        own_ref[...] = left
        send_ref[...] = right

    @pl.when(jnp.logical_not(first))
    def _():
        own_ref[...] = right
        send_ref[...] = left

    acc_gain[0:1, :] += d_gain_a
    acc_gain[1:2, :] += d_gain_b
    acc_gain[2:3, :] += d_gain_p
    acc_gain[3:4, :] += d_query

    @pl.when(step == pl.num_programs(0) - 1)
    def _():
        w = width
        down = acc_down[...].astype(BF16).T
        grads_ref[0 : 2 * w, 0:w] = down[0 : 2 * w]
        grads_ref[0 : 2 * w, w : 2 * w] = down[2 * w : 4 * w]
        up = acc_up[...].astype(BF16)
        grads_ref[2 * w : 3 * w, :] = up[:, : 2 * w]
        grads_ref[3 * w : 4 * w, :] = up[:, 2 * w :]
        qkv_g = acc_qkv[...].astype(BF16)
        grads_ref[4 * w : 5 * w, :] = qkv_g[:, : 2 * w]
        grads_ref[5 * w : 6 * w, 0:w] = qkv_g[:, 2 * w :]
        grads_ref[5 * w : 6 * w, w : 2 * w] = acc_out[...].astype(BF16)
        gains_ref[...] = acc_gain[...]


def whole(array):
    return pl.BlockSpec(array.shape, lambda *_: (0,) * array.ndim)


def char_forward(section, chars, lens, weights):
    slots, width = chars.shape[1:]
    words = chars.shape[0] // 2
    rows = words * slots
    steps = words // BLOCK_WORDS
    block = BLOCK_WORDS * slots
    w_proj = weights[-1]
    hidden = weights[4].shape[1]

    def out(n):
        return pl.BlockSpec((block, n), lambda i, s: (i, 0))

    return pl.pallas_call(
        char_forward_kernel,
        grid_spec=pltpu.PrefetchScalarGridSpec(
            num_scalar_prefetch=1,
            grid=(steps,),
            in_specs=[
                pl.BlockSpec((BLOCK_WORDS, slots, width), lambda i, s: (s[0] * steps + i, 0, 0)),
                pl.BlockSpec((1,) + lens.shape[1:], lambda i, s: (s[0] * steps + i, 0, 0)),
            ]
            + [whole(w) for w in weights],
            out_specs=[
                out(3 * width), out(width), out(width), out(hidden), out(width),
                pl.BlockSpec((BLOCK_WORDS, width), lambda i, s: (i, 0)),
                pl.BlockSpec((BLOCK_WORDS, w_proj.shape[1]), lambda i, s: (i, 0)),
            ],
        ),
        out_shape=[
            jax.ShapeDtypeStruct((rows, 3 * width), BF16),
            jax.ShapeDtypeStruct((rows, width), BF16),
            jax.ShapeDtypeStruct((rows, width), F32),
            jax.ShapeDtypeStruct((rows, hidden), BF16),
            jax.ShapeDtypeStruct((rows, width), F32),
            jax.ShapeDtypeStruct((words, width), BF16),
            jax.ShapeDtypeStruct((words, w_proj.shape[1]), BF16),
        ],
        compiler_params=pltpu.CompilerParams(vmem_limit_bytes=50 << 20),
        name="char_forward",
    )(section, chars, lens, *weights)


def word_pass(vector, mask, grad, pooled, weights, w_proj):
    rows, width = vector.shape
    total = sum(w.size for w in weights if w.shape[0] > 1) // width
    operands = (vector, mask, grad, pooled) + weights + (w_proj,)
    return pl.pallas_call(
        word_kernel,
        out_shape=[
            jax.ShapeDtypeStruct((rows, width), BF16),
            jax.ShapeDtypeStruct((total, width), BF16),
            jax.ShapeDtypeStruct((8, width), F32),
            jax.ShapeDtypeStruct(w_proj.shape, BF16),
            jax.ShapeDtypeStruct((rows, w_proj.shape[0]), F32),
        ],
        compiler_params=pltpu.CompilerParams(vmem_limit_bytes=56 << 20),
        name="word_pass",
    )(*operands)


def char_backward(section, chars, lens, gpool, saved, weights):
    slots, width = chars.shape[1:]
    words = chars.shape[0] // 2
    steps = words // BLOCK_WORDS
    block = BLOCK_WORDS * slots
    hidden = weights[4].shape[1]

    def rowed(n):
        return pl.BlockSpec((block, n), lambda i, s: (i, 0))

    half = pl.BlockSpec((BLOCK_WORDS, slots, width // 2), lambda i, s: (i, 0, 0))
    total = (hidden * 2 + 4 * width) // 2
    return pl.pallas_call(
        char_backward_kernel,
        grid_spec=pltpu.PrefetchScalarGridSpec(
            num_scalar_prefetch=1,
            grid=(steps,),
            in_specs=[
                pl.BlockSpec((BLOCK_WORDS, slots, width), lambda i, s: (s[0] * steps + i, 0, 0)),
                pl.BlockSpec((1,) + lens.shape[1:], lambda i, s: (s[0] * steps + i, 0, 0)),
                pl.BlockSpec((BLOCK_WORDS, width), lambda i, s: (i, 0)),
                rowed(3 * width), rowed(width), rowed(width), rowed(hidden), rowed(width),
            ]
            + [whole(w) for w in weights],
            out_specs=[
                half, half,
                pl.BlockSpec((total, 2 * width), lambda i, s: (0, 0)),
                pl.BlockSpec((8, width), lambda i, s: (0, 0)),
            ],
            scratch_shapes=[
                pltpu.VMEM((width, hidden), F32),
                pltpu.VMEM((width, hidden), F32),
                pltpu.VMEM((width, width), F32),
                pltpu.VMEM((width, 3 * width), F32),
                pltpu.VMEM((8, width), F32),
            ],
        ),
        out_shape=[
            jax.ShapeDtypeStruct((words, slots, width // 2), BF16),
            jax.ShapeDtypeStruct((words, slots, width // 2), BF16),
            jax.ShapeDtypeStruct((total, 2 * width), BF16),
            jax.ShapeDtypeStruct((8, width), F32),
        ],
        compiler_params=pltpu.CompilerParams(vmem_limit_bytes=50 << 20),
        name="char_backward",
    )(section, chars, lens, gpool, *saved, *weights)


AXES = ("section", "dp")


def exchange(value, partner):
    dp = lax.axis_size("dp")
    pairs = []
    for s in range(lax.axis_size("section")):
        for d in range(dp):
            t, e = partner(s, d)
            pairs.append((s * dp + d, t * dp + e))
    return lax.ppermute(value, AXES, pairs)


def by_core(first, second):
    return lambda s, d: first(s, d) if d % 2 == 0 else second(s, d)


def flip_section(s, d):
    return 1 - s, d


def flip_bit(bit):
    return lambda s, d: (s, d ^ (1 << bit))


def sum_all(value):
    sec = lax.axis_index("section")
    dp = lax.axis_index("dp")
    core = dp & 1
    x = (dp >> 1) & 1
    bits = lax.axis_size("dp").bit_length() - 1
    stages = [
        (flip_bit(0), core),
        (by_core(flip_bit(1), flip_section), jnp.where(core == 0, x, sec)),
        (by_core(flip_section, flip_bit(1)), jnp.where(core == 0, sec, x)),
        (flip_bit(2), (dp >> 2) & 1),
        (flip_bit(3), (dp >> 3) & 1),
    ]
    for partner, bit in stages:
        n = value.shape[0] // 2
        keep = lax.dynamic_slice_in_dim(value, bit * n, n, 0)
        send = lax.dynamic_slice_in_dim(value, (1 - bit) * n, n, 0)
        value = (keep.astype(F32) + exchange(send, partner).astype(F32)).astype(BF16)
    for extra in range(4, bits):
        value = (value.astype(F32) + exchange(value, flip_bit(extra)).astype(F32)).astype(BF16)
    for partner, bit in reversed(stages):
        other = exchange(value, partner)
        value = jnp.concatenate(
            [jnp.where(bit == 0, value, other), jnp.where(bit == 0, other, value)], axis=0
        )
    return value


def body(
    chars, char_lengths, word_mask, out_grad, char_gain_a, char_qkv, char_out, char_gain_b, char_up,
    char_down, pool_gain, pool_query, char_proj, word_gain_a, word_qkv, word_out, word_gain_b,
    word_up, word_down,
):
    def flat(v):
        return v.reshape(1, -1)

    slots, cwidth = chars.shape[1:]
    words = chars.shape[0] // 2
    width = word_qkv.shape[0]
    sec = lax.axis_index("section")
    section = sec.astype(jnp.int32).reshape(1)
    lens = jnp.repeat(char_lengths, slots).reshape(-1, BLOCK_WORDS * slots // GROUP, GROUP)
    char_weights = (
        flat(char_gain_a), char_qkv, char_out, flat(char_gain_b), char_up, char_down,
        flat(pool_gain), flat(pool_query), char_proj,
    )
    word_weights = (flat(word_gain_a), word_qkv, word_out, flat(word_gain_b), word_up, word_down)
    *saved, pooled, vector = char_forward(section, chars, lens, char_weights)
    mask = lax.dynamic_slice_in_dim(word_mask, sec * words, words).reshape(1, words)
    grad = lax.dynamic_slice_in_dim(out_grad, sec * words, words, 0)
    result, word_grads, word_gains, proj_grad, gpool = word_pass(
        vector, mask, grad, pooled, word_weights, char_proj
    )
    word_sum = sum_all(word_grads).astype(F32)
    half = width // 2
    own_out = jnp.where(sec == 0, result[:, :half], result[:, half:])
    send_out = jnp.where(sec == 0, result[:, half:], result[:, :half])
    got_out = exchange(send_out, flip_section)
    word_outputs = jnp.concatenate(
        [jnp.where(sec == 0, own_out, got_out), jnp.where(sec == 0, got_out, own_out)], axis=0
    )
    own, send, char_grads, char_gains = char_backward(
        section, chars, lens, gpool, saved, char_weights[:-1]
    )
    got = exchange(send, flip_section)
    char_grad = jnp.concatenate([jnp.where(sec == 0, own, got), jnp.where(sec == 0, got, own)], axis=0)
    gains = jnp.concatenate([word_gains, char_gains.reshape(-1, width)], axis=0)
    rows = proj_grad.shape[0] + char_grads.shape[0] + gains.shape[0]
    pad = jnp.zeros((-rows % 512, width), BF16)
    rest = sum_all(jnp.concatenate([proj_grad, char_grads, gains.astype(BF16), pad], axis=0)).astype(F32)
    hidden = word_up.shape[1]
    d_word_down = word_sum[:hidden]
    at = hidden
    d_word_up = jnp.concatenate([word_sum[at + j * width : at + (j + 1) * width] for j in range(hidden // width)], axis=1)
    at += hidden
    d_word_out = word_sum[at : at + width]
    at += width
    d_word_qkv = jnp.concatenate([word_sum[at + j * width : at + (j + 1) * width] for j in range(3)], axis=1)
    w = cwidth
    d_proj = rest[:w]
    rest = rest[w:]
    d_down = jnp.concatenate([rest[: 2 * w, :w], rest[: 2 * w, w:]], axis=0)
    d_up = jnp.concatenate([rest[2 * w : 3 * w], rest[3 * w : 4 * w]], axis=1)
    d_qkv = jnp.concatenate([rest[4 * w : 5 * w], rest[5 * w : 6 * w, :w]], axis=1)
    d_out = rest[5 * w : 6 * w, w:]
    gains = rest[6 * w :]
    cg = gains[8:12].reshape(-1, w)
    return (
        word_outputs, char_grad, cg[0], d_qkv, d_out, cg[1], d_up, d_down, cg[2], cg[3], d_proj,
        gains[0], d_word_qkv, d_word_out, gains[1], d_word_up, d_word_down,
    )


def solution(mesh):
    return jax.shard_map(
        body,
        mesh=mesh,
        in_specs=(P("dp", None, None), P("dp"), P("dp"), P("dp", None)) + (P(),) * 15,
        out_specs=(P("dp", "section"), P("dp", None, "section")) + (P(),) * 15,
        check_vma=False,
    )
```

```python
import functools

import jax
import jax.numpy as jnp
from jax import lax
from jax.experimental import pallas as pl
from jax.experimental.pallas import tpu as pltpu
from jax.sharding import PartitionSpec as P

CHEADS = 4
WHEADS = 8
EPSILON = 1e-06
NEGATIVE = -1e30
GROUP = 128
F32 = jnp.float32
BF16 = jnp.bfloat16
C0 = 0.7978845608028654
C1 = 0.7978845608028654 * 0.044715


def mm(left, right):
    return jnp.dot(left, right, preferred_element_type=F32)


def mm_nt(left, right):
    return lax.dot_general(left, right, (((1,), (1,)), ((), ())), preferred_element_type=F32)


def mm_tn(left, right):
    return lax.dot_general(left, right, (((0,), (0,)), ((), ())), preferred_element_type=F32)


def inverse_rms(value):
    return lax.rsqrt(jnp.mean(value * value, axis=-1, keepdims=True) + EPSILON)


def gelu(u):
    t = jnp.tanh(u * (C0 + C1 * (u * u)))
    half = 0.5 * u
    return half + half * t


def gelu_both(u):
    square = u * u
    t = jnp.tanh(u * (C0 + C1 * square))
    half = 0.5 * u
    slope = (0.5 + 0.5 * t) + half * (1.0 - t * t) * (C0 + (3.0 * C1) * square)
    return half + half * t, slope


def rms_back(unit, inverse, gain, grad):
    scaled = grad * gain
    d_value = inverse * (scaled - unit * jnp.mean(scaled * unit, axis=-1, keepdims=True))
    return d_value, jnp.sum(grad * unit, axis=0, keepdims=True)


def two_heads(pair):
    lane = lax.broadcasted_iota(jnp.int32, pair.shape, 1)
    zero = jnp.zeros_like(pair)
    return jnp.concatenate(
        [jnp.where(lane < 64, pair, zero), jnp.where(lane < 64, zero, pair)], axis=0
    )


def side(stacked):
    n = stacked.shape[0] // 2
    return jnp.concatenate([stacked[:n], stacked[n:]], axis=1)


BLOCK_WORDS = 64

def row_mean(value):
    return jnp.mean(value, axis=-1, keepdims=True)


def inverse_rms(value):
    return lax.rsqrt(row_mean(value * value) + EPSILON)


def low_gelu(u):
    square = u * u
    t = jnp.tanh(u * (BF16(C0) + BF16(C1) * square))
    half = BF16(0.5) * u
    return half + half * t


def compact(full, lane_word):
    out = full[0:16]
    for w in range(1, 8):
        out = jnp.where(lane_word == w, full[16 * w : 16 * w + 16], out)
    return out


def spread(small, diagonal):
    return jnp.concatenate([small] * 8, axis=0) * diagonal


def diagonal_mask():
    row = lax.broadcasted_iota(jnp.int32, (GROUP, GROUP), 0)
    lane = lax.broadcasted_iota(jnp.int32, (GROUP, GROUP), 1)
    return jnp.where((row // 16) == (lane // 16), 1.0, 0.0).astype(BF16)


def pool_weights(normed, query, lens):
    rows, width = normed.shape
    words = rows // 16
    score = mm_nt(jnp.broadcast_to(query, (words, width)), normed) * width ** (-0.5)
    at = lax.broadcasted_iota(jnp.int32, (words, rows), 0)
    lane = lax.broadcasted_iota(jnp.int32, (words, rows), 1)
    own = lane // 16 == at
    slot = (lane % 16).astype(F32)
    score = jnp.where(own & (slot < lens[0:1]), score, NEGATIVE)
    e = jnp.exp(score - jnp.max(score, axis=1, keepdims=True))
    return e * (1.0 / jnp.sum(e, axis=1, keepdims=True)), own


def word_step(
    ids_ref, e_ref, mask_ref, g_ref, pooled_ref, gain_c_ref, gain_d_ref, w_qkv, w_out, w_up, w_down, w_proj,
    own_ref, send_ref, keep1, send1, keep2, send2, gains_ref, proj_ref, gpool_ref,
):
    rows, width = e_ref.shape
    hidden = w_up.shape[1]
    core = ids_ref[1]

    def place(which, keep, send, at, value):
        value = value.astype(BF16)

        @pl.when(core == which)
        def _():
            keep[at : at + value.shape[0], :] = value

        @pl.when(core != which)
        def _():
            send[at : at + value.shape[0], :] = value

    y = e_ref[...].astype(F32)
    gain_c, gain_d = gain_row(gain_c_ref), gain_row(gain_d_ref)
    own_mask = mask_ref[...].reshape(1, 2 * rows)
    own_mask = jnp.where(ids_ref[0] == 0, own_mask[:, :rows], own_mask[:, rows:])
    inv_c = inverse_rms(y)
    unit_c = y * inv_c
    a3 = (unit_c * gain_c).astype(BF16)
    qkv = mm(a3, w_qkv[...]).astype(BF16)
    row = lax.broadcasted_iota(jnp.int32, (rows, rows), 0)
    lane = lax.broadcasted_iota(jnp.int32, (rows, rows), 1)
    allowed = (lane <= row) & (own_mask > 0)
    mask = jnp.where(allowed, 0.0, NEGATIVE)
    mask = jnp.concatenate([mask, mask], axis=0)
    pairs = width // 128
    probs, mixed = [], []
    for j in range(pairs):
        q = qkv[:, j * 128 : j * 128 + 128] * 0.125
        k = qkv[:, width + j * 128 : width + j * 128 + 128]
        v = qkv[:, 2 * width + j * 128 : 2 * width + j * 128 + 128]
        s = mm_nt(two_heads(q), k) + mask
        e = jnp.exp(s - jnp.max(s, axis=-1, keepdims=True))
        p = e * (1.0 / jnp.sum(e, axis=-1, keepdims=True))
        probs.append(p)
        mixed.append(mm(side(p.astype(BF16)), two_heads(v)).astype(BF16))
    o2 = jnp.concatenate(mixed, axis=1)
    y1 = y + mm(o2, w_out[...])
    inv_d = inverse_rms(y1)
    unit_d = y1 * inv_d
    a4 = (unit_d * gain_d).astype(BF16)
    h2, slope = low_gelu_both(mm(a4, w_up[...]).astype(BF16))
    result = (y1 + mm(h2, w_down[...])).astype(BF16)

    @pl.when(ids_ref[0] == 0)
    def _():
        own_ref[...] = result[:, : width // 2]
        send_ref[...] = result[:, width // 2 :]

    @pl.when(ids_ref[0] != 0)
    def _():
        own_ref[...] = result[:, width // 2 :]
        send_ref[...] = result[:, : width // 2]

    g = g_ref[...]
    place(0, keep1, send1, 0, mm_tn(h2, g))
    g_u2 = slope * mm_nt(g, w_down[...]).astype(BF16)
    for j in range(hidden // width):
        place(1, keep1, send1, j * width, mm_tn(a4, g_u2[:, j * width : (j + 1) * width]))
    d_y1n, d_gain_d = rms_back_mean(unit_d, inv_d, gain_d, mm_nt(g_u2, w_up[...]))
    g_y1 = g.astype(F32) + d_y1n
    g_b1 = g_y1.astype(BF16)
    place(1, keep2, send2, width, mm_tn(o2, g_b1))
    g_o2 = mm_nt(g_b1, w_out[...]).astype(BF16)
    d_q, d_k, d_v = [], [], []
    for j in range(pairs):
        q = qkv[:, j * 128 : j * 128 + 128] * 0.125
        k = qkv[:, width + j * 128 : width + j * 128 + 128]
        v = qkv[:, 2 * width + j * 128 : 2 * width + j * 128 + 128]
        go = two_heads(g_o2[:, j * 128 : j * 128 + 128])
        p = probs[j]
        g_p = mm_nt(go, v)
        d_v.append(mm_tn(p.astype(BF16), go).astype(BF16))
        d_s = (p * (g_p - jnp.sum(g_p * p, axis=-1, keepdims=True))).astype(BF16)
        d_q.append((mm(side(d_s), two_heads(k)) * 0.125).astype(BF16))
        d_k.append(mm_tn(d_s, two_heads(q)).astype(BF16))
    g_qkv = jnp.concatenate(d_q + d_k + d_v, axis=1)
    place(0, keep2, send2, 0, mm_tn(a3, g_qkv[:, :width]))
    place(0, keep2, send2, width, mm_tn(a3, g_qkv[:, width : 2 * width]))
    place(1, keep2, send2, 0, mm_tn(a3, g_qkv[:, 2 * width :]))
    d_yn, d_gain_c = rms_back_mean(unit_c, inv_c, gain_c, mm_nt(g_qkv, w_qkv[...]))
    g_e = (g_y1 + d_yn).astype(BF16)
    gains_ref[0:1, :] = d_gain_c
    gains_ref[1:2, :] = d_gain_d
    gains_ref[2:8, :] = jnp.zeros((6, width), F32)
    proj_ref[...] = mm_tn(pooled_ref[...], g_e).astype(BF16)
    gpool_ref[...] = mm_nt(g_e, w_proj[...]).astype(BF16)


def low_gelu_both(u):
    square = u * u
    t = jnp.tanh(u * (BF16(C0) + BF16(C1) * square))
    half = BF16(0.5) * u
    slope = (BF16(0.5) + BF16(0.5) * t) + half * (BF16(1.0) - t * t) * (BF16(C0) + BF16(3.0 * C1) * square)
    return half + half * t, slope


def rms_back_mean(unit, inverse, gain, grad):
    scaled = grad * gain
    d_value = inverse * (scaled - unit * row_mean(scaled * unit))
    return d_value, jnp.sum(grad * unit, axis=0, keepdims=True)


def lens_lanes(lens_ref, first, words):
    n = lens_ref.shape[0]
    row = jnp.broadcast_to(lens_ref[...].reshape(1, n), (8, n)).astype(F32)
    row = pltpu.roll(row, n - first, 1)[:, :GROUP].astype(BF16)
    at = lax.broadcasted_iota(jnp.int32, (GROUP, 16 * words), 0)
    lane = lax.broadcasted_iota(jnp.int32, (GROUP, 16 * words), 1)
    return mm(row, jnp.where(at == lane // 16, 1.0, 0.0).astype(BF16))


def gain_row(ref):
    return ref[...].astype(F32).reshape(1, ref.shape[0])


def char_step(
    x, lens, gain_a, w_qkv, w_out, gain_b, w_up, w_down, gain_p, query_p, w_proj,
    qkv_out, o1_out, x1_out, u1_out, x2_out, probs_out,
):
    rows, width = x.shape
    words = rows // 16
    a1 = (x * inverse_rms(x) * gain_row(gain_a)).astype(BF16)
    qkv_out[...] = mm(a1, w_qkv[...]).astype(BF16)
    lane_word = lax.broadcasted_iota(jnp.int32, (16, GROUP), 1) // 16
    key_slot = lax.broadcasted_iota(jnp.int32, (16, GROUP), 0).astype(F32)
    diagonal = diagonal_mask()
    groups = rows // GROUP
    scores = []
    for g in range(groups):
        at = slice(g * GROUP, (g + 1) * GROUP)
        mask = jnp.where(key_slot < lens[0:1, at], 0.0, NEGATIVE)
        for j in range(2):
            q = qkv_out[at, j * 128 : j * 128 + 128] * 0.125
            k = qkv_out[at, width + j * 128 : width + j * 128 + 128]
            s = mm_nt(two_heads(k), q)
            scores.append(compact(s[:GROUP], lane_word) + mask)
            scores.append(compact(s[GROUP:], lane_word) + mask)
    scores = jnp.stack(scores)
    e = jnp.exp(scores - jnp.max(scores, axis=1, keepdims=True))
    p = e * (1.0 / jnp.sum(e, axis=1, keepdims=True))
    probs_out[...] = p
    p = p.astype(BF16)
    for g in range(groups):
        at = slice(g * GROUP, (g + 1) * GROUP)
        for j in range(2):
            v = qkv_out[at, 2 * width + j * 128 : 2 * width + j * 128 + 128]
            i = 4 * g + 2 * j
            both = jnp.concatenate([spread(p[i], diagonal), spread(p[i + 1], diagonal)], axis=0)
            o1_out[at, j * 128 : j * 128 + 128] = mm_tn(both, two_heads(v)).astype(BF16)
    x1 = x + mm(o1_out[...], w_out[...])
    x1_out[...] = x1
    a2 = (x1 * inverse_rms(x1) * gain_row(gain_b)).astype(BF16)
    u1 = mm(a2, w_up[...]).astype(BF16)
    u1_out[...] = u1
    x2 = x1 + mm(low_gelu(u1), w_down[...])
    x2_out[...] = x2
    normed = (x2 * inverse_rms(x2) * gain_row(gain_p)).astype(BF16)
    weights, _ = pool_weights(normed, gain_row(query_p).astype(BF16), lens)
    pooled = mm(weights.astype(BF16), normed).astype(BF16)
    return pooled, mm(pooled, w_proj[...]).astype(BF16)


def forward_kernel(
    steps, ids_ref, chars, lens_ref, mask_ref, g_ref,
    gain_a, w_qkv, w_out, gain_b, w_up, w_down, gain_p, query_p, w_proj,
    word_gain_a, word_gain_b, hbm_qkv, hbm_out, hbm_up, hbm_down,
    own_ref, send_ref, keep1, send1, keep2, send2, gains_ref, proj_ref, gpool_ref, *rest,
):
    saved, rest = rest[:6], rest[6:]
    slots, rest = rest[:6], rest[6:]
    e_all, pooled_all, ww_qkv, ww_out, ww_up, ww_down, save_sem, load_sem = rest
    step = pl.program_id(0)
    words, count, width = chars.shape
    rows = words * count
    loads = [
        pltpu.make_async_copy(a, b, load_sem.at[i])
        for i, (a, b) in enumerate(((hbm_qkv, ww_qkv), (hbm_out, ww_out), (hbm_up, ww_up), (hbm_down, ww_down)))
    ]

    def saves(at):
        slot = at % 2
        out = []
        for i, (a, b) in enumerate(zip(slots, saved)):
            n = a.shape[1]
            out.append(pltpu.make_async_copy(a.at[slot], b.at[pl.ds(at * n, n)], save_sem.at[slot, i]))
        return out

    @pl.when(step == 0)
    def _():
        for c in loads:
            c.start()

    @pl.when(step < steps)
    def _():
        @pl.when(step >= 2)
        def _():
            for c in saves(step - 2):
                c.wait()

        slot = step % 2
        lens = lens_lanes(lens_ref, ids_ref[0] * (steps * words) + step * words, words)
        pooled, e = char_step(
            chars[...].reshape(rows, width).astype(F32), lens,
            gain_a, w_qkv, w_out, gain_b, w_up, w_down, gain_p, query_p, w_proj,
            *[s.at[slot] for s in slots],
        )
        pooled_all[pl.ds(step * words, words), :] = pooled
        e_all[pl.ds(step * words, words), :] = e
        for c in saves(step):
            c.start()

    @pl.when(step == steps)
    def _():
        for c in loads:
            c.wait()
        word_step(
            ids_ref, e_all, mask_ref, g_ref, pooled_all, word_gain_a, word_gain_b, ww_qkv, ww_out, ww_up, ww_down, w_proj,
            own_ref, send_ref, keep1, send1, keep2, send2, gains_ref, proj_ref, gpool_ref,
        )
        for at in range(max(0, steps - 2), steps):
            for c in saves(jnp.int32(at)):
                c.wait()


def ffn_backward_kernel(
    part, parts, ids_ref, lens_ref, gpool, x1_in, u1_in, x2_in, gain_b, gain_p, query_p, w_up, w_down, proj_ref, *rest,
):
    first, last = part == 0, part == parts - 1
    before = [] if first else rest[:3]
    if last:
        g_x1_out, keep_ref, sent_ref, acc_gain, acc_down, acc_up = rest[-6:]
    else:
        g_x1_out, acc_gain, acc_down, acc_up = rest[-4:]
    accs = (acc_gain, acc_down, acc_up)
    step = pl.program_id(0)
    steps = pl.num_programs(0)
    words, width = gpool.shape
    rows = words * 16

    lens = lens_lanes(lens_ref, ((ids_ref[0] * parts + part) * steps + step) * words, words)
    gain_pf = gain_row(gain_p)
    x2 = x2_in[...]
    inv_p = inverse_rms(x2)
    unit_p = x2 * inv_p
    normed = (unit_p * gain_pf).astype(BF16)
    query = gain_row(query_p).astype(BF16)
    weights, own = pool_weights(normed, query, lens)
    gp = gpool[...]
    g_w = jnp.where(own, mm_nt(gp, normed), 0.0)
    g_r = weights * (g_w - jnp.sum(weights * g_w, axis=1, keepdims=True)) * width ** (-0.5)
    left = jnp.concatenate([weights, g_r], axis=0).astype(BF16)
    right = jnp.concatenate([gp, jnp.broadcast_to(query, gp.shape)], axis=0)
    g_n = mm_tn(left, right)
    d_query = jnp.sum(mm(left[words:], normed), axis=0, keepdims=True)
    g_x2, d_gain_p = rms_back_mean(unit_p, inv_p, gain_pf, g_n)
    g_b2 = g_x2.astype(BF16)
    h1, slope = low_gelu_both(u1_in[...])
    d_down = mm_tn(g_b2, h1)
    g_u1 = slope * mm_nt(g_b2, w_down[...]).astype(BF16)
    gain_bf = gain_row(gain_b)
    x1 = x1_in[...]
    inv_b = inverse_rms(x1)
    unit_b = x1 * inv_b
    d_up = mm_tn((unit_b * gain_bf).astype(BF16), g_u1)
    d_x1n, d_gain_b = rms_back_mean(unit_b, inv_b, gain_bf, mm_nt(g_u1, w_up[...]))
    g_x1_out[...] = g_x2 + d_x1n
    gains = jnp.concatenate([jnp.zeros_like(d_gain_b), d_gain_b, d_gain_p, d_query, jnp.zeros((4, width), F32)], axis=0)

    @pl.when(step == 0)
    def _():
        for i, (acc, value) in enumerate(zip(accs, (gains, d_down, d_up))):
            acc[...] = value if first else before[i][...] + value

    @pl.when(step > 0)
    def _():
        for acc, value in zip(accs, (gains, d_down, d_up)):
            acc[...] += value

    if not last:
        return

    @pl.when(step == steps - 1)
    def _():
        w = width

        def fill(zero, one):
            up = acc_up[...].astype(BF16)
            zero[0:w, :] = up[:, : 2 * w]
            zero[w : 2 * w, :] = up[:, 2 * w :]
            zero[2 * w :, :] = proj_ref[: w // 2]
            down = acc_down[...].astype(BF16).T
            one[0 : 2 * w, 0:w] = down[0 : 2 * w]
            one[0 : 2 * w, w : 2 * w] = down[2 * w : 4 * w]
            one[2 * w :, :] = proj_ref[w // 2 :]

        @pl.when(ids_ref[1] == 0)
        def _():
            fill(keep_ref, sent_ref)

        @pl.when(ids_ref[1] != 0)
        def _():
            fill(sent_ref, keep_ref)


def attention_backward_kernel(
    part, parts, ids_ref, chars, g_x1_in, qkv_in, o1_in, probs_in, gain_a, w_qkv, w_out, *rest,
):
    rest = list(rest)
    first, last = part == 0, part == parts - 1
    if not first:
        rest.pop(0)
    before = [] if first else rest[:3]
    char_gains, word_gains = (rest[3:5] if not first else rest[:2]) if last else (None, None)
    if last:
        char_grad, send_ref, keep_ref, sent_ref, *accs, g_qkv, own_buf, own_sem = rest[-10:]
    else:
        char_grad, send_ref, *accs, g_qkv, own_buf, own_sem = rest[-8:]
    acc_out, acc_qkv, acc_gain = accs
    step = pl.program_id(0)
    steps = pl.num_programs(0)
    words, slots, width = chars.shape
    rows = words * slots
    sec = ids_ref[0]
    g_x1 = g_x1_in[...]
    g_c1 = g_x1.astype(BF16)
    d_out = mm_tn(o1_in[...], g_c1)
    g_o1 = mm_nt(g_c1, w_out[...]).astype(BF16)
    lane_word = lax.broadcasted_iota(jnp.int32, (16, GROUP), 1) // 16
    diagonal = diagonal_mask()
    groups = rows // GROUP
    g_probs = []
    for g in range(groups):
        at = slice(g * GROUP, (g + 1) * GROUP)
        for j in range(2):
            v = qkv_in[at, 2 * width + j * 128 : 2 * width + j * 128 + 128]
            full = mm_nt(two_heads(v), g_o1[at, j * 128 : j * 128 + 128])
            g_probs.append(compact(full[:GROUP], lane_word))
            g_probs.append(compact(full[GROUP:], lane_word))
    g_probs = jnp.stack(g_probs)
    p = probs_in[...]
    d_s = (p * (g_probs - jnp.sum(g_probs * p, axis=1, keepdims=True))).astype(BF16)
    p = p.astype(BF16)
    for g in range(groups):
        at = slice(g * GROUP, (g + 1) * GROUP)
        for j in range(2):
            cols = j * 128
            q = qkv_in[at, cols : cols + 128] * 0.125
            k = qkv_in[at, width + cols : width + cols + 128]
            go = g_o1[at, cols : cols + 128]
            i = 4 * g + 2 * j
            p_wide = jnp.concatenate([spread(p[i], diagonal), spread(p[i + 1], diagonal)], axis=1)
            s0, s1 = spread(d_s[i], diagonal), spread(d_s[i + 1], diagonal)
            g_qkv[at, 2 * width + cols : 2 * width + cols + 128] = mm(p_wide, two_heads(go)).astype(BF16)
            g_qkv[at, width + cols : width + cols + 128] = mm(
                jnp.concatenate([s0, s1], axis=1), two_heads(q)
            ).astype(BF16)
            g_qkv[at, cols : cols + 128] = (
                mm_tn(jnp.concatenate([s0, s1], axis=0), two_heads(k)) * 0.125
            ).astype(BF16)
    gain_af = gain_row(gain_a)
    x = chars[...].reshape(rows, width).astype(F32)
    inv_a = inverse_rms(x)
    unit_a = x * inv_a
    d_qkv = mm_tn((unit_a * gain_af).astype(BF16), g_qkv[...])
    d_xn, d_gain_a = rms_back_mean(unit_a, inv_a, gain_af, mm_nt(g_qkv[...], w_qkv[...]))
    d_gain = jnp.concatenate([d_gain_a, jnp.zeros((7, width), F32)], axis=0)

    @pl.when(step == 0)
    def _():
        for i, (acc, value) in enumerate(zip(accs, (d_out, d_qkv, d_gain))):
            acc[...] = value if first else before[i][...] + value

    @pl.when(step > 0)
    def _():
        for acc, value in zip(accs, (d_out, d_qkv, d_gain)):
            acc[...] += value

    d_chars = (g_x1 + d_xn).astype(BF16).reshape(words, slots, width)
    left, right = d_chars[:, :, : width // 2], d_chars[:, :, width // 2 :]

    def own_copy(at):
        spot = ((sec * parts + part) * steps + at) * words
        return pltpu.make_async_copy(own_buf, char_grad.at[pl.ds(spot, words)], own_sem)

    @pl.when(step > 0)
    def _():
        own_copy(step - 1).wait()

    @pl.when(sec == 0)
    def _():
        own_buf[...] = left
        send_ref[...] = right

    @pl.when(sec != 0)
    def _():
        own_buf[...] = right
        send_ref[...] = left

    own_copy(step).start()

    @pl.when(step == steps - 1)
    def _():
        own_copy(step).wait()

    if last:

        @pl.when(step == steps - 1)
        def _():
            w = width

            def fill(zero, one):
                qkv_g = acc_qkv[...].astype(BF16)
                zero[0:w, :] = qkv_g[:, : 2 * w]
                gains = acc_gain[...] + char_gains[...]
                zero[w : w + 16, :] = jnp.concatenate(
                    [word_gains[...], jnp.concatenate([gains, gains], axis=1)], axis=0
                ).astype(BF16)
                zero[w + 16 :, :] = jnp.zeros((w // 4 - 16, 2 * w), BF16)
                one[0:w, 0:w] = qkv_g[:, 2 * w :]
                one[0:w, w : 2 * w] = acc_out[...].astype(BF16)
                one[w:, :] = jnp.zeros((w // 4, 2 * w), BF16)

            @pl.when(ids_ref[1] == 0)
            def _():
                fill(keep_ref, sent_ref)

            @pl.when(ids_ref[1] != 0)
            def _():
                fill(sent_ref, keep_ref)


def whole(array):
    return pl.BlockSpec(array.shape, lambda *_: (0,) * array.ndim)


ANY = pl.BlockSpec(memory_space=pl.ANY)
VMEM = pltpu.CompilerParams(vmem_limit_bytes=56 << 20)
SMALL = pltpu.CompilerParams(vmem_limit_bytes=24 << 20)
BACK = pltpu.CompilerParams(vmem_limit_bytes=40 << 20)


def shaped(shape, dtype):
    return jax.ShapeDtypeStruct(shape, dtype)


class Order:
    last = None


def ordered(kernel, scalars, inputs, grid, in_specs, out_specs, out_shape, token=0, scratch_shapes=(), **options):
    extra = () if Order.last is None else (Order.last,)
    out = pl.pallas_call(
        kernel,
        grid_spec=pltpu.PrefetchScalarGridSpec(
            num_scalar_prefetch=len(scalars),
            grid=grid,
            in_specs=list(in_specs) + [ANY] * len(extra),
            out_specs=out_specs,
            scratch_shapes=list(scratch_shapes),
        ),
        out_shape=out_shape,
        **options,
    )(*scalars, *inputs, *extra)
    Order.last = out[token] if isinstance(out, (list, tuple)) else out
    return out


def cost(micros):
    return pl.CostEstimate(flops=int(micros * 10000000000.0), bytes_accessed=1 << 20, transcendentals=0)


def forward(ids, chars, lens, mask, grad, char_weights, word_gains, word_weights):
    slots, width = chars.shape[1:]
    words = chars.shape[0] // 2
    rows = words * slots
    steps = words // BLOCK_WORDS
    block = BLOCK_WORDS * slots
    hidden = char_weights[4].shape[1]
    w_proj = char_weights[-1]
    word_width = w_proj.shape[1]
    word_hidden = word_weights[2].shape[1]
    outs = [
        shaped((words, word_width // 2), BF16),
        shaped((words, word_width // 2), BF16),
        shaped((word_hidden, word_width), BF16),
        shaped((word_hidden, word_width), BF16),
        shaped((2 * word_width, word_width), BF16),
        shaped((2 * word_width, word_width), BF16),
        shaped((8, word_width), F32),
        shaped(w_proj.shape, BF16),
        shaped((words, width), BF16),
    ]
    kinds = [((3 * width,), BF16), ((width,), BF16), ((width,), F32), ((hidden,), BF16), ((width,), F32)]
    saved = [shaped((rows,) + tail, dtype) for tail, dtype in kinds] + [shaped((rows // 32, 16, GROUP), F32)]
    slot_shapes = [pltpu.VMEM((2, v.shape[0] // steps) + v.shape[1:], v.dtype) for v in saved]
    inputs = (lens, mask, grad) + tuple(char_weights) + tuple(word_gains)
    specs = [whole(v) for v in inputs]
    specs[2] = pl.BlockSpec((words, word_width), lambda i, s: (s[0], 0))
    return pl.pallas_call(
        functools.partial(forward_kernel, steps),
        grid_spec=pltpu.PrefetchScalarGridSpec(
            num_scalar_prefetch=1,
            grid=(steps + 1,),
            in_specs=[
                pl.BlockSpec(
                    (BLOCK_WORDS, slots, width), lambda i, s: (s[0] * steps + jnp.minimum(i, steps - 1), 0, 0)
                )
            ]
            + specs
            + [ANY] * 4,
            out_specs=[whole(v) for v in outs] + [ANY] * 6,
            scratch_shapes=slot_shapes
            + [pltpu.VMEM((words, word_width), BF16), pltpu.VMEM((words, width), BF16)]
            + [pltpu.VMEM(v.shape, BF16) for v in word_weights]
            + [pltpu.SemaphoreType.DMA((2, 6)), pltpu.SemaphoreType.DMA((4,))],
        ),
        out_shape=outs + saved,
        compiler_params=VMEM,
        cost_estimate=cost(35),
        name="forward",
    )(ids, chars, *inputs, *word_weights)


def ffn_backward(ids, part, parts, lens, gpool, x1, u1, x2, gains, weights, proj, before):
    words, width = gpool.shape
    all_steps = words // BLOCK_WORDS
    steps = all_steps // parts
    first = part * steps
    last = part == parts - 1
    hidden = weights[0].shape[1]
    inputs = (lens, gpool, x1, u1, x2) + tuple(gains) + tuple(weights) + (proj,)

    def cut(v, offset):
        return pl.BlockSpec((v.shape[0] // all_steps,) + v.shape[1:], lambda i, s: (offset + i,) + (0,) * (v.ndim - 1))

    specs = [whole(v) for v in inputs]
    for i in range(1, 5):
        specs[i] = cut(inputs[i], first)
    specs += [whole(v) for v in before]
    accs = [shaped((8, width), F32), shaped((width, hidden), F32), shaped((width, hidden), F32)]
    g_x1 = shaped((x1.shape[0] // parts, width), F32)
    tail = [shaped((2 * width + width // 2, 2 * width), BF16)] * 2 + accs[:1] if last else accs
    return ordered(
        functools.partial(ffn_backward_kernel, part, parts),
        (ids,),
        inputs + tuple(before),
        grid=(steps,),
        in_specs=specs,
        out_specs=[pl.BlockSpec((g_x1.shape[0] // steps, width), lambda i, s: (i, 0))] + [whole(v) for v in tail],
        scratch_shapes=[pltpu.VMEM(v.shape, F32) for v in accs[1:]] if last else [],
        out_shape=[g_x1] + tail,
        token=1 if last else 1,
        compiler_params=VMEM,
        cost_estimate=cost(24 / parts),
        name="ffn_backward_%d" % part,
    )


def attention_backward(ids, part, parts, chars, g_x1, qkv, o1, probs, gain, weights, carried, before, extra):
    slots, width = chars.shape[1:]
    words = chars.shape[0] // 2
    all_steps = words // BLOCK_WORDS
    steps = all_steps // parts
    first = part * steps
    last = part == parts - 1

    def cut(v):
        return pl.BlockSpec((v.shape[0] // all_steps,) + v.shape[1:], lambda i, s: (first + i,) + (0,) * (v.ndim - 1))

    inputs = (chars, g_x1, qkv, o1, probs, gain) + tuple(weights)
    specs = [whole(v) for v in inputs]
    specs[0] = pl.BlockSpec((BLOCK_WORDS, slots, width), lambda i, s: (s[0] * all_steps + first + i, 0, 0))
    for i in range(2, 5):
        specs[i] = cut(inputs[i])
    specs[1] = pl.BlockSpec((g_x1.shape[0] // steps, width), lambda i, s: (i, 0))
    aliases = {1 + len(inputs): 0} if carried else {}
    inputs += tuple(carried) + tuple(before) + tuple(extra)
    specs += [ANY] * len(carried) + [whole(v) for v in before] + [whole(v) for v in extra]
    accs = [shaped(v, F32) for v in ((width, width), (width, 3 * width), (8, width))]
    half = pl.BlockSpec((BLOCK_WORDS, slots, width // 2), lambda i, s: (i, 0, 0))
    outs = [shaped(chars.shape[:2] + (width // 2,), BF16), shaped((words // parts, slots, width // 2), BF16)]
    scratch = [
        pltpu.VMEM((BLOCK_WORDS * slots, 3 * width), BF16),
        pltpu.VMEM((BLOCK_WORDS, slots, width // 2), BF16),
        pltpu.SemaphoreType.DMA,
    ]
    if last:
        tail = [shaped((width + width // 4, 2 * width), BF16)] * 2
        scratch = [pltpu.VMEM(v.shape, F32) for v in accs] + scratch
    else:
        tail = accs
    return ordered(
        functools.partial(attention_backward_kernel, part, parts),
        (ids,),
        inputs,
        grid=(steps,),
        in_specs=specs,
        out_specs=[ANY, half] + [whole(v) for v in tail],
        scratch_shapes=scratch,
        out_shape=outs + tail,
        token=2 if last else 4,
        input_output_aliases=aliases,
        compiler_params=VMEM,
        cost_estimate=cost(20 / parts),
        name="attention_backward_%d" % part,
    )


AXES = ("section", "dp")


def exchange(value, partner):
    dp = lax.axis_size("dp")
    pairs = []
    for s in range(lax.axis_size("section")):
        for d in range(dp):
            t, e = partner(s, d)
            pairs.append((s * dp + d, t * dp + e))
    return lax.ppermute(value, AXES, pairs)


def by_core(first, second):
    return lambda s, d: first(s, d) if d % 2 == 0 else second(s, d)


def flip_section(s, d):
    return 1 - s, d


def flip_bit(bit):
    return lambda s, d: (s, d ^ (1 << bit))


def combine_kernel(bit_ref, keep_a, keep_b, got_a, got_b, *rest):
    keep, send = rest[-2:]
    keep[...] = (keep_a[...].astype(F32) + got_a[...].astype(F32)).astype(BF16)
    send[...] = (keep_b[...].astype(F32) + got_b[...].astype(F32)).astype(BF16)


def combine(keep, got, bit):
    rows, width = keep.shape
    half = rows // 2
    steps = 4 if half % 64 == 0 and half >= 512 else 1
    block = half // steps
    mine = pl.BlockSpec((block, width), lambda i, b: (b[0] * steps + i, 0))
    other = pl.BlockSpec((block, width), lambda i, b: ((1 - b[0]) * steps + i, 0))
    out = pl.BlockSpec((block, width), lambda i, b: (i, 0))
    return ordered(
        combine_kernel,
        (bit.reshape(1),),
        (keep, keep, got, got),
        grid=(steps,),
        in_specs=[mine, other, mine, other],
        out_specs=[out, out],
        out_shape=[shaped((half, width), BF16)] * 2,
        compiler_params=SMALL,
        cost_estimate=cost(0.5 + rows * width * 6 / 3e6),
        name="combine",
    )


def add_kernel(mine, got, *rest):
    rest[-1][...] = (mine[...].astype(F32) + got[...].astype(F32)).astype(BF16)


def add(mine, got):
    return ordered(
        add_kernel,
        (),
        (mine, got),
        grid=(1,),
        in_specs=[whole(mine)] * 2,
        out_specs=whole(mine),
        out_shape=shaped(mine.shape, mine.dtype),
        compiler_params=SMALL,
        cost_estimate=cost(0.6),
        name="add",
    )


def join_kernel(bit_ref, mine, got, *rest):
    rest[-1][...] = jnp.where(pl.program_id(0) == bit_ref[0], mine[...], got[...])


def join(mine, got, bit):
    rows = mine.shape[0]
    steps = max(1, min(2, mine.size // 2**18))
    block = (rows // steps,) + mine.shape[1:]
    zeros = (0,) * (mine.ndim - 1)
    half = pl.BlockSpec(block, lambda h, i, b: (i,) + zeros)
    return ordered(
        join_kernel,
        (bit.reshape(1),),
        (mine, got),
        grid=(2, steps),
        in_specs=[half, half],
        out_specs=pl.BlockSpec(block, lambda h, i, b: (h * steps + i,) + zeros),
        out_shape=shaped((2 * rows,) + mine.shape[1:], mine.dtype),
        cost_estimate=cost(1.0),
        compiler_params=SMALL,
        name="join",
    )


def spots():
    sec = lax.axis_index("section").astype(jnp.int32)
    dp = lax.axis_index("dp").astype(jnp.int32)
    core = dp & 1
    x = (dp >> 1) & 1
    return [
        (by_core(flip_bit(1), flip_section), jnp.where(core == 0, x, sec)),
        (by_core(flip_section, flip_bit(1)), jnp.where(core == 0, sec, x)),
        (flip_bit(2), (dp >> 2) & 1),
        (flip_bit(3), (dp >> 3) & 1),
    ]


def finish_down_up_kernel(ids_ref, mine, other, *rest):
    core = ids_ref[1]
    down, up = rest[-2:]
    down[...] = jnp.where(core == 0, mine[...], other[...]).astype(F32)
    up[...] = jnp.where(core == 0, other[...], mine[...]).astype(F32)


def finish_down_up(ids, mine, other):
    hidden, width = mine.shape
    steps = hidden // width
    block = pl.BlockSpec((width, width), lambda i, s: (i, 0))
    return ordered(
        finish_down_up_kernel,
        (ids,),
        (mine, other),
        grid=(steps,),
        in_specs=[block, block],
        out_specs=[block, pl.BlockSpec((width, width), lambda i, s: (0, i))],
        out_shape=[shaped((hidden, width), F32), shaped((width, hidden), F32)],
        compiler_params=SMALL,
        cost_estimate=cost(4),
        name="finish_down_up",
    )


def finish_qkv_out_kernel(ids_ref, mine, other, *rest):
    core = ids_ref[1]
    width = mine.shape[1]
    qkv_ref, out_ref = rest[-2:]

    def fill(zero, one):
        qkv_ref[:, :width] = zero[:width].astype(F32)
        qkv_ref[:, width : 2 * width] = zero[width:].astype(F32)
        qkv_ref[:, 2 * width :] = one[:width].astype(F32)
        out_ref[...] = one[width:].astype(F32)

    @pl.when(core == 0)
    def _():
        fill(mine, other)

    @pl.when(core != 0)
    def _():
        fill(other, mine)


def finish_qkv_out(ids, mine, other):
    width = mine.shape[1]
    outs = [shaped((width, 3 * width), F32), shaped((width, width), F32)]
    return ordered(
        finish_qkv_out_kernel,
        (ids,),
        (mine, other),
        grid=(1,),
        in_specs=[whole(mine)] * 2,
        out_specs=[whole(v) for v in outs],
        out_shape=outs,
        token=1,
        compiler_params=SMALL,
        cost_estimate=cost(3),
        name="finish_qkv_out",
    )


def finish_ffn_kernel(ids_ref, mine, other, *rest):
    up, down, proj = rest[-3:]
    w = mine.shape[1] // 2

    def fill(zero, one):
        up[:, : 2 * w] = zero[0:w].astype(F32)
        up[:, 2 * w :] = zero[w : 2 * w].astype(F32)
        proj[0 : w // 2] = zero[2 * w :].astype(F32)
        proj[w // 2 :] = one[2 * w :].astype(F32)
        down[0 : 2 * w] = one[0 : 2 * w, 0:w].astype(F32)
        down[2 * w : 4 * w] = one[0 : 2 * w, w : 2 * w].astype(F32)

    @pl.when(ids_ref[1] == 0)
    def _():
        fill(mine, other)

    @pl.when(ids_ref[1] != 0)
    def _():
        fill(other, mine)


def finish_attention_kernel(ids_ref, mine, other, *rest):
    qkv, out, gains = rest[-3:]
    w = mine.shape[1] // 2

    def fill(zero, one):
        gains[...] = zero[w : w + 16].astype(F32)
        qkv[:, : 2 * w] = zero[0:w].astype(F32)
        qkv[:, 2 * w :] = one[0:w, :w].astype(F32)
        out[...] = one[0:w, w:].astype(F32)

    @pl.when(ids_ref[1] == 0)
    def _():
        fill(mine, other)

    @pl.when(ids_ref[1] != 0)
    def _():
        fill(other, mine)


def finish_char(kernel, shapes, ids, mine, other):
    outs = [shaped(v, F32) for v in shapes]
    return ordered(
        kernel,
        (ids,),
        (mine, other),
        grid=(1,),
        in_specs=[whole(mine)] * 2,
        out_specs=[whole(v) for v in outs],
        out_shape=outs,
        token=1,
        compiler_params=SMALL,
        cost_estimate=cost(2),
        name="finish_char",
    )


PARTS = 2
CUTS = {'1': 2, '2': 2, '3': 2, '4': 2}
ORDER = ('2', '1', 'o', 'f0', '1', '2', 'f1', '1', '2', '3', 'a0', '1', '2', '3', 'a1', '3', '4', '2', '3', 'e0', '4', '2', '1', '4', '3', 'e1', '4', '2', '3', '1', '2', '4', '3', '4', '3', '4', '1', '4', '1')


def place_kernel(ids_ref, held, got, *rest):
    rest[-1][...] = got[...]


def place_rows(ids, part, parts, held, got):
    zeros = (0,) * (held.ndim - 1)
    return ordered(
        place_kernel,
        (ids,),
        (held, got),
        grid=(1,),
        in_specs=[ANY, whole(got)],
        out_specs=pl.BlockSpec(got.shape, lambda i, s: ((1 - s[0]) * parts + part,) + zeros),
        out_shape=shaped(held.shape, held.dtype),
        input_output_aliases={1: 0},
        cost_estimate=cost(1.5),
        compiler_params=SMALL,
        name="place_rows",
    )


def summing(keep, send, cuts):
    bits = lax.axis_size("dp").bit_length() - 1
    stages = spots()
    got = exchange(send, flip_bit(0))
    yield None
    for partner, bit in stages[:cuts]:
        keep, send = combine(keep, got, bit)
        got = exchange(send, partner)
        yield None
    value = add(keep, got)
    for more in list(range(cuts, 4)) + list(range(4, bits)):
        got = exchange(value, flip_bit(more))
        yield None
        value = add(value, got)
    for partner, bit in reversed(stages[:cuts]):
        got = exchange(value, partner)
        yield None
        value = join(value, got, bit)
    yield value, exchange(value, flip_bit(0))


def body(
    chars, char_lengths, word_mask, out_grad, char_gain_a, char_qkv, char_out, char_gain_b, char_up,
    char_down, pool_gain, pool_query, char_proj, word_gain_a, word_qkv, word_out, word_gain_b,
    word_up, word_down,
):
    Order.last = None
    cwidth = chars.shape[2]
    sec = lax.axis_index("section").astype(jnp.int32)
    ids = jnp.stack([sec, lax.axis_index("dp").astype(jnp.int32) & 1])
    own_out, send_out, keep1, send1, keep2, send2, d_word_gains, d_proj_part, gpool, *saved = forward(
        ids, chars, char_lengths, word_mask, out_grad,
        (char_gain_a, char_qkv, char_out, char_gain_b, char_up, char_down, pool_gain, pool_query, char_proj),
        (word_gain_a, word_gain_b), (word_qkv, word_out, word_up, word_down),
    )
    qkv, o1, x1, u1, x2, probs = saved
    ffn_args = (
        char_lengths, gpool, x1, u1, x2, (char_gain_b, pool_gain, pool_query), (char_up, char_down), d_proj_part
    )
    args = (qkv, o1, probs, char_gain_a, (char_qkv, char_out))
    w = cwidth
    chains, done, kept = {}, {}, {}

    def total(name, keep, send, cuts, finish):
        def chain():
            for out in summing(keep, send, cuts):
                if out is None:
                    yield
            done[name] = finish(ids, *out)

        chains[name] = chain()
        next(chains[name])

    def swap(name, send, finish):
        def chain():
            got = exchange(send, flip_section)
            yield
            done[name] = finish(got)

        chains[name] = chain()
        next(chains[name])

    def place(part):
        def finish(got):
            kept["grad"] = place_rows(ids, part, PARTS, kept["grad"], got)

        return finish

    def step(name):
        if name == "f0":
            kept["f0"], *kept["f"] = ffn_backward(ids, 0, PARTS, *ffn_args, ())
        elif name == "f1":
            kept["f1"], keep, send, kept["gains"] = ffn_backward(ids, 1, PARTS, *ffn_args, kept["f"])
            shapes = ((w, 4 * w), (4 * w, w), (w, 2 * w))
            total("3", keep, send, CUTS["3"], functools.partial(finish_char, finish_ffn_kernel, shapes))
        elif name == "a0":
            kept["grad"], send, *kept["a"] = attention_backward(ids, 0, PARTS, chars, kept["f0"], *args, (), (), ())
            swap("e0", send, place(0))
        elif name == "a1":
            kept["grad"], send, keep4, send4 = attention_backward(
                ids, 1, PARTS, chars, kept["f1"], *args, (kept["grad"],), kept["a"], (kept["gains"], d_word_gains)
            )
            shapes = ((w, 3 * w), (w, w), (16, 2 * w))
            total("4", keep4, send4, CUTS["4"], functools.partial(finish_char, finish_attention_kernel, shapes))
            swap("e1", send, place(1))
        else:
            next(chains[name], None)

    total("1", keep1, send1, CUTS["1"], finish_down_up)
    total("2", keep2, send2, CUTS["2"], finish_qkv_out)
    swap("o", send_out, lambda got: join(own_out, got, sec))
    for name in ORDER:
        step(name)
    while len(done) < len(chains):
        for name in chains:
            step(name)
    word_outputs, char_grad = done["o"], kept["grad"]
    d_word_down, d_word_up = done["1"]
    d_word_qkv, d_word_out = done["2"]
    d_up, d_down, d_proj = done["3"]
    d_qkv, d_out, gains = done["4"]
    return (
        word_outputs, char_grad, gains[8, :cwidth], d_qkv, d_out, gains[9, :cwidth], d_up, d_down,
        gains[10, :cwidth], gains[11, :cwidth], d_proj, gains[0], d_word_qkv, d_word_out, gains[1],
        d_word_up, d_word_down,
    )


def solution(mesh):
    return jax.shard_map(
        body,
        mesh=mesh,
        in_specs=(P("dp", None, None), P("dp"), P("dp"), P("dp", None)) + (P(),) * 15,
        out_specs=(P("dp", "section"), P("dp", None, "section")) + (P(),) * 15,
        check_vma=False,
    )
```
